256 devices in a mesh: row: 8 (over z), col: 8 (over y_lo, x), mat: 4 (over y_hi, core).
Axes of the slice: x: 4, y: 4 (y_hi: 2, y_lo: 2; y = y_hi * 2 + y_lo), z: 8, core: 2. Of those that a mesh axis runs over, the one named last changes fastest.
Arguments:
- iterate: bfloat16 [14336, 8192], P(('mat', 'row', 'col')), parts along dimension 0, may hold values from -4 to 4, as said below
Outputs:
- update: bfloat16 [14336, 8192], P(('mat', 'row', 'col')), parts along dimension 0
The draws below stay inside these ranges and needn't reach their ends.
There are 4 independent parts, one for each index of `mat`. The reference program is written for one: setup_inputs(seed, part) draws one part's arguments, and reference() takes and returns one part's arrays. A program takes and returns all parts, laid end to end along the dimension named above; each array names one. Nothing has to cross between parts.
Inputs may be any that keep to these rules, and one draw needn't show every extreme that they name: Real-valued iterate entries.
All inputs are finite; a program needn't handle non-finite values.
Results may differ from the reference program's by a relative error of at most 0.0038.
Values may be sent and summed in bfloat16 or wider, within the bound.
No kernel may reach another device: no remote copies, remote signals or barrier semaphores. Data moves between devices by JAX's collectives and lax.ppermute only.
A program may use at most 64 MiB of HBM per device.

```python
import math
import jax
import jax.numpy as jnp

ROWS = 3584
COLS = 8192


def draw_iterate(key, part):
    key = jax.random.fold_in(key, 7)
    subkeys = jax.random.split(key, 3)
    row_low, row_high, col_low, col_high = (0.1, 1.0, 0.15, 1.5)
    noise_part = jnp.clip(jax.random.normal(subkeys[2], (ROWS, COLS)), -4.0, 4.0)
    row_scale = row_low * jnp.exp(jax.random.uniform(subkeys[0], (ROWS, 1)) * math.log(row_high / row_low))
    col_scale = col_low * jnp.exp(jax.random.uniform(subkeys[1], (1, COLS)) * math.log(col_high / col_low))
    values = noise_part * row_scale * col_scale
    return jnp.clip(values, -4.0, 4.0).astype(jnp.bfloat16)


def setup_inputs(seed: int = 0, part: int = 0) -> dict:
    key_of = jax.random.split(jax.random.key(seed), 2)
    own_keys = jax.random.split(jax.random.fold_in(key_of[1], part), 2)
    return {
        "iterate": draw_iterate(jax.random.fold_in(jax.random.fold_in(key_of[1], part), 71), part),
    }


def reference(iterate):
    inverse_cols = 1.0 / COLS
    gram = (jnp.dot(iterate, iterate.T, preferred_element_type=jnp.float32) * inverse_cols).astype(jnp.bfloat16)
    square = jnp.dot(gram, gram, preferred_element_type=jnp.float32)
    poly = (-4.7750 * gram.astype(jnp.float32) + 2.0315 * square).astype(jnp.bfloat16)
    product = jnp.dot(poly, iterate, preferred_element_type=jnp.float32)
    return (3.4445 * iterate.astype(jnp.float32) + product).astype(jnp.bfloat16)
```

```python
import jax
import jax.numpy as jnp
from jax import lax
from jax.sharding import PartitionSpec as P

AXES = ("row", "col", "mat")
N = 8
MIXED = True
SUM_TYPE = jnp.float32


def ring_to_col(p):
    return p if p < 4 else 11 - p


def place(mat, r, q):
    if MIXED and mat % 2 == 1:
        r, q = q, r
    return (r * 8 + ring_to_col(q)) * 4 + mat


def shift_perm(dr, dq):
    return [
        (place(m, r, q), place(m, (r + dr) % N, (q + dq) % N))
        for m in range(4)
        for r in range(N)
        for q in range(N)
    ]


def send(x, dr=0, dq=0):
    return lax.ppermute(x, AXES, shift_perm(dr, dq))


def shift(x, axis, by):
    return send(x, dr=by) if axis == "r" else send(x, dq=by)


def roll_blocks(x, by):
    return lax.dynamic_slice_in_dim(jnp.concatenate([x, x], 0), by, N, 0)


def ring_gather(x, axis):
    half = x.shape[0] // 2
    out = [None] * N
    out[0] = x
    up, down = x, x
    for s in (1, 2, 3):
        up = shift(up, axis, 1)
        down = shift(down, axis, -1)
        out[N - s] = up
        out[s] = down
    first = shift(up[:half], axis, 1)
    second = shift(down[half:], axis, -1)
    out[4] = jnp.concatenate([first, second], 0)
    return out


def ring_sum(parts):
    nb = parts.shape[0]
    half = (nb + 1) // 2

    def term(t):
        return parts[:, t % N]

    def sent(x, by):
        return shift(x.astype(SUM_TYPE), "q", by).astype(jnp.float32)

    zero = jnp.zeros_like(term(0))
    up = jnp.concatenate([sent(term(4)[:half], 1), zero[half:]], 0)
    if nb > half:
        down = jnp.concatenate([zero[:half], sent(term(4)[half:], -1)], 0)
    else:
        down = zero
    for t in (3, 2, 1):
        up = sent(term(t) + up, 1)
        down = sent(term(-t) + down, -1)
    return term(0) + up + down


def body(iterate):
    m, cols = iterate.shape
    width = cols // N
    f32, bf16 = jnp.float32, jnp.bfloat16
    z = lax.axis_index("row")
    col = lax.axis_index("col")
    ring = jnp.where(col < 4, col, 11 - col)
    if MIXED:
        odd = lax.axis_index("mat") % 2 == 1
        r = jnp.where(odd, ring, z)
        q = jnp.where(odd, z, ring)
    else:
        r, q = z, ring

    blocks = roll_blocks(iterate.reshape(m, N, width).transpose(1, 0, 2), q)
    own = [blocks[0]] + [None] * (N - 1)
    for t in range(1, N):
        own[N - t] = send(blocks[t], dq=t)
    own = jnp.stack(own, 0)
    own_abs = roll_blocks(own, (N - q) % N).reshape(N * m, width)
    own = own.reshape(N * m, width)

    panel = ring_gather(own, "r")

    contract = (((1,), (1,)), ((), ()))
    sums = [None] * N
    for group in ((0, 1, 7), (2, 6), (3, 5, 4)):
        parts = jnp.stack(
            [
                lax.dot_general(panel[d], own_abs, contract, preferred_element_type=f32).reshape(
                    N, m, N * m
                )
                for d in group
            ],
            0,
        )
        total = ring_sum(parts)
        for i, d in enumerate(group):
            sums[d] = total[i]
    gram = (jnp.stack(sums, 0) * (1.0 / cols)).astype(bf16)
    by_t = jnp.stack([p.reshape(N, m, width) for p in panel], 1).reshape(N, N * m, width)

    gram_abs = roll_blocks(gram, (N - r) % N).reshape(N * m, N * m)
    size = N * m
    row_id = lax.broadcasted_iota(jnp.int32, (size, size), 0)
    col_id = lax.broadcasted_iota(jnp.int32, (size, size), 1)
    turn = (col_id == (row_id + m * q) % size).astype(bf16)
    turned = lax.dot_general(turn, gram_abs, contract, preferred_element_type=f32).astype(bf16)

    over_q = ring_gather(gram, "q")
    over_r = ring_gather(turned, "r")
    right = jnp.stack(over_q, 1).reshape(N * size, size)
    left = jnp.concatenate(over_r, 0)
    lead = (((0,), (0,)), ((), ()))
    square = lax.dot_general(left, right, lead, preferred_element_type=f32)
    poly = (-4.775 * gram_abs.astype(f32) + 2.0315 * square).astype(bf16)
    poly = roll_blocks(poly.reshape(N, m, size), r)

    polys = ring_gather(poly, "q")
    product = 3.4445 * own_abs.astype(f32)
    for t in (0, 1, 7, 2, 6, 3, 5, 4):
        product = product + lax.dot_general(
            polys[t].reshape(size, size), by_t[t], lead, preferred_element_type=f32
        )
    update = roll_blocks(product.astype(bf16).reshape(N, m, width), q)
    back = [update[0]] + [None] * (N - 1)
    for t in range(1, N):
        back[N - t] = send(update[t], dq=t)
    out = roll_blocks(jnp.stack(back, 0), (N - q) % N)
    return out.transpose(1, 0, 2).reshape(m, cols)


def solution(mesh):
    spec = P(("mat", "row", "col"), None)
    return jax.shard_map(body, mesh=mesh, in_specs=(spec,), out_specs=spec, check_vma=False)
```

```python
import jax
import jax.numpy as jnp
from jax import lax
from jax.sharding import PartitionSpec as P

AXES = ("row", "col", "mat")
N = 8
MIXED = False
XS = 1
GS = 1
SUM_TYPE = jnp.bfloat16
ORDER = (0, 1, 7, 2, 6, 3, 5, 4)
F32, BF16 = jnp.float32, jnp.bfloat16
ROWS_BY_ROWS = (((1,), (1,)), ((), ()))
COLS_BY_COLS = (((0,), (0,)), ((), ()))


def ring_to_col(p):
    return p if p < 4 else 11 - p


def place(mat, r, q):
    if MIXED and mat % 2 == 1:
        r, q = q, r
    return (r * 8 + ring_to_col(q)) * 4 + mat


def shift(x, axis, by):
    dr, dq = (by, 0) if axis == "r" else (0, by)
    pairs = [
        (place(m, r, q), place(m, (r + dr) % N, (q + dq) % N))
        for m in range(4)
        for r in range(N)
        for q in range(N)
    ]
    return lax.ppermute(x, AXES, pairs)


def dot(a, b, dims=(((1,), (0,)), ((), ()))):
    return lax.dot_general(a, b, dims, preferred_element_type=F32)


def ring_gather(x, axis, streams=1):
    if streams > 1:
        w = x.shape[1] // streams
        got = [ring_gather(x[:, i * w : (i + 1) * w], axis) for i in range(streams)]
        return [jnp.concatenate([g[d] for g in got], 1) for d in range(N)]
    half = x.shape[1] // 2
    out = [None] * N
    out[0] = x
    up, down = x, x
    for s in (1, 2, 3):
        up = shift(up, axis, 1)
        down = shift(down, axis, -1)
        out[N - s] = up
        out[s] = down
    first = shift(up[:, :half], axis, 1)
    second = shift(down[:, half:], axis, -1)
    out[4] = jnp.concatenate([first, second], 1)
    return out


def ring_sum(term, axis):
    last = term(4)
    half = last.shape[1] // 2

    def sent(x, by):
        return shift(x.astype(SUM_TYPE), axis, by).astype(F32)

    first = sent(last[:, :half], 1)
    second = sent(last[:, half:], -1)
    up, down = term(3), term(5)
    up = jnp.concatenate([up[:, :half] + first, up[:, half:]], 1)
    down = jnp.concatenate([down[:, :half], down[:, half:] + second], 1)
    for d in (2, 1):
        up = sent(up, 1) + term(d)
        down = sent(down, -1) + term(N - d)
    return term(0) + sent(up, 1) + sent(down, -1)


def body(iterate):
    m, cols = iterate.shape
    size = N * m
    z = lax.axis_index("row")
    col = lax.axis_index("col")
    ring = jnp.where(col < 4, col, 11 - col)
    if MIXED:
        odd = lax.axis_index("mat") % 2 == 1
        r = jnp.where(odd, ring, z)
        q = jnp.where(odd, z, ring)
    else:
        r, q = z, ring

    arrival = lax.broadcasted_iota(jnp.int32, (N, m, size), 0)
    distance = jnp.zeros_like(arrival)
    for p, d in enumerate(ORDER):
        distance = jnp.where(arrival == p, d, distance)
    row = lax.broadcasted_iota(jnp.int32, (N, m, size), 1)
    target = lax.broadcasted_iota(jnp.int32, (N, m, size), 2)

    def turn(at):
        return ((distance + at) % N * m + row == target).astype(BF16).reshape(size, size)

    turn_q, turn_r = lax.optimization_barrier((turn(q), turn(r)))
    over_q = ring_gather(iterate, "q")
    over_r = ring_gather(iterate, "r", XS)
    right = jnp.concatenate([over_q[d] for d in ORDER[:7]], 0)
    left = jnp.concatenate([over_r[d] for d in ORDER[:7]], 0)
    tile = jnp.concatenate(
        [
            jnp.concatenate(
                [dot(left, right, ROWS_BY_ROWS), dot(left, over_q[4], ROWS_BY_ROWS)], 1
            ),
            jnp.concatenate(
                [dot(over_r[4], right, ROWS_BY_ROWS), dot(over_r[4], over_q[4], ROWS_BY_ROWS)], 1
            ),
        ],
        0,
    )
    tile = (tile * (1.0 / cols)).astype(BF16)
    right = jnp.concatenate([right, over_q[4]], 0)
    left = jnp.concatenate([left, over_r[4]], 0)

    tile_q = dot(tile, turn_q).astype(BF16)
    turned = dot(tile, turn_r, COLS_BY_COLS).astype(BF16)
    gram = dot(turned, turn_q, COLS_BY_COLS).astype(BF16)

    gram_q = ring_gather(tile_q, "q")
    gram_r = ring_gather(turned, "r", GS)
    stack = jnp.stack([gram_q[d].reshape(N, m, size) for d in ORDER], 1).reshape(N, size, size)
    square = jnp.zeros((size, size), F32)
    for p, d in enumerate(ORDER):
        square = square + dot(gram_r[d], stack[p], COLS_BY_COLS)
    poly = (-4.775 * gram.astype(F32) + 2.0315 * square).astype(BF16)
    poly = lax.optimization_barrier(poly)
    poly = dot(turn_r, poly).astype(BF16)
    poly_r = dot(poly, turn_q, ROWS_BY_ROWS).astype(BF16)
    poly_q = dot(turn_q, poly, ROWS_BY_ROWS).astype(BF16)

    split = cols // 2

    def terms(a, x):
        first = dot(a[7 * m :], x)
        pairs = [dot(a[p * m : (p + 2) * m], x) for p in (5, 3, 1)]
        own = dot(a[:m], x)
        made = {0: own, 4: first}
        for p, y in zip((5, 3, 1), pairs):
            made[ORDER[p]], made[ORDER[p + 1]] = y[:m], y[m:]
        return made.__getitem__

    term_q = terms(poly_q, left[:, :split])
    term_r = terms(poly_r, right[:, split:])

    product = jnp.concatenate([ring_sum(term_q, "q"), ring_sum(term_r, "r")], 1)
    return (3.4445 * iterate.astype(F32) + product).astype(BF16)


def solution(mesh):
    spec = P(("mat", "row", "col"), None)
    return jax.shard_map(body, mesh=mesh, in_specs=(spec,), out_specs=spec, check_vma=False)
```

```python
import jax
import jax.numpy as jnp
from jax import lax
from jax.sharding import PartitionSpec as P

AXES = ("row", "col", "mat")
N = 8
MIXED = False
SUM_TYPE = jnp.bfloat16
ORDER = (0, 1, 7, 2, 6, 3, 5, 4)
F32, BF16 = jnp.float32, jnp.bfloat16
ROWS_BY_ROWS = (((1,), (1,)), ((), ()))
COLS_BY_COLS = (((0,), (0,)), ((), ()))


def ring_to_col(p):
    return p if p < 4 else 11 - p


def place(mat, r, q):
    if MIXED and mat % 2 == 1:
        r, q = q, r
    return (r * 8 + ring_to_col(q)) * 4 + mat


def shift(x, axis, by):
    dr, dq = (by, 0) if axis == "r" else (0, by)
    pairs = [
        (place(m, r, q), place(m, (r + dr) % N, (q + dq) % N))
        for m in range(4)
        for r in range(N)
        for q in range(N)
    ]
    return lax.ppermute(x, AXES, pairs)


def dot(a, b, dims=(((1,), (0,)), ((), ()))):
    return lax.dot_general(a, b, dims, preferred_element_type=F32)


def ring_gather(x, axis):
    by = 1 if x.shape[1] > 128 else 0
    half = x.shape[by] // 2
    out = [None] * N
    out[0] = x
    up, down = x, x
    for s in (1, 2, 3):
        up = shift(up, axis, 1)
        down = shift(down, axis, -1)
        out[N - s] = up
        out[s] = down
    first = shift(lax.slice_in_dim(up, 0, half, axis=by), axis, 1)
    second = shift(lax.slice_in_dim(down, half, 2 * half, axis=by), axis, -1)
    out[4] = jnp.concatenate([first, second], by)
    return out


def pack(x):
    n, w = x.shape
    full, rest = w // 128, w % 128
    if rest != 64:
        return x
    tail = x[:, full * 128 :]
    tail = jnp.concatenate([tail[: n // 2], tail[n // 2 :]], 1)
    return jnp.concatenate([x[:, i * 128 : (i + 1) * 128] for i in range(full)] + [tail], 0)


def unpack(x, n, w):
    full, rest = w // 128, w % 128
    if rest != 64:
        return x
    tail = x[full * n :]
    tail = jnp.concatenate([tail[:, :64], tail[:, 64:]], 0)
    return jnp.concatenate([x[i * n : (i + 1) * n] for i in range(full)] + [tail], 1)


def ring_gather_tile(x, axis):
    n, w = x.shape
    got = ring_gather(pack(x), axis)
    return [x] + [unpack(g, n, w) for g in got[1:]]


def ring_sum(term, axis):
    last = term(4)
    half = last.shape[1] // 2

    def sent(x, by):
        return shift(x.astype(SUM_TYPE), axis, by).astype(F32)

    first = sent(last[:, :half], 1)
    second = sent(last[:, half:], -1)
    up, down = term(3), term(5)
    up = jnp.concatenate([up[:, :half] + first, up[:, half:]], 1)
    down = jnp.concatenate([down[:, :half], down[:, half:] + second], 1)
    for d in (2, 1):
        up = sent(up, 1) + term(d)
        down = sent(down, -1) + term(N - d)
    return term(0) + sent(up, 1) + sent(down, -1)


def body(iterate):
    m, cols = iterate.shape
    size = N * m
    z = lax.axis_index("row")
    col = lax.axis_index("col")
    ring = jnp.where(col < 4, col, 11 - col)
    if MIXED:
        odd = lax.axis_index("mat") % 2 == 1
        r = jnp.where(odd, ring, z)
        q = jnp.where(odd, z, ring)
    else:
        r, q = z, ring

    arrival = lax.broadcasted_iota(jnp.int32, (N, m, size), 0)
    distance = jnp.zeros_like(arrival)
    for p, d in enumerate(ORDER):
        distance = jnp.where(arrival == p, d, distance)
    row = lax.broadcasted_iota(jnp.int32, (N, m, size), 1)
    target = lax.broadcasted_iota(jnp.int32, (N, m, size), 2)

    def turn(at):
        return ((distance + at) % N * m + row == target).astype(BF16).reshape(size, size)

    turn_q, turn_r = lax.optimization_barrier((turn(q), turn(r)))
    over_q = ring_gather(iterate, "q")
    over_r = ring_gather(iterate, "r")
    seven = 7 * m
    space = jnp.zeros((m, cols), BF16)
    right = jnp.concatenate([over_q[d] for d in ORDER[:7]] + [space], 0)
    left = jnp.concatenate([over_r[d] for d in ORDER[:7]] + [space], 0)
    most = dot(left[:seven], right[:seven], ROWS_BY_ROWS)
    right = lax.dynamic_update_slice(right, over_q[4], (seven, 0))
    left = lax.dynamic_update_slice(left, over_r[4], (seven, 0))
    side = dot(left[:seven], over_q[4], ROWS_BY_ROWS)
    below = dot(over_r[4], right, ROWS_BY_ROWS)
    tile = jnp.concatenate([jnp.concatenate([most, side], 1), below], 0)
    tile = (tile * (1.0 / cols)).astype(BF16)

    tile_q = dot(tile, turn_q).astype(BF16)
    turned = dot(tile, turn_r, COLS_BY_COLS).astype(BF16)
    gram = dot(turned, turn_q, COLS_BY_COLS).astype(BF16)

    gram_q = ring_gather_tile(tile_q, "q")
    gram_r = ring_gather_tile(turned, "r")
    stack = jnp.stack([gram_q[d].reshape(N, m, size) for d in ORDER], 1).reshape(N, size, size)
    square = jnp.zeros((size, size), F32)
    for p, d in enumerate(ORDER):
        square = square + dot(gram_r[d], stack[p], COLS_BY_COLS)
    poly = (-4.775 * gram.astype(F32) + 2.0315 * square).astype(BF16)
    poly = lax.optimization_barrier(poly)
    poly = dot(turn_r, poly).astype(BF16)
    poly_r = dot(poly, turn_q, ROWS_BY_ROWS).astype(BF16)
    poly_q = dot(turn_q, poly, ROWS_BY_ROWS).astype(BF16)

    split = cols // 2

    def terms(a, x):
        first = dot(a[7 * m :], x)
        pairs = [dot(a[p * m : (p + 2) * m], x) for p in (5, 3, 1)]
        own = dot(a[:m], x)
        made = {0: own, 4: first}
        for p, y in zip((5, 3, 1), pairs):
            made[ORDER[p]], made[ORDER[p + 1]] = y[:m], y[m:]
        return made.__getitem__

    term_q = terms(poly_q, left[:, :split])
    term_r = terms(poly_r, right[:, split:])

    product = jnp.concatenate([ring_sum(term_q, "q"), ring_sum(term_r, "r")], 1)
    return (3.4445 * iterate.astype(F32) + product).astype(BF16)


def solution(mesh):
    spec = P(("mat", "row", "col"), None)
    return jax.shard_map(body, mesh=mesh, in_specs=(spec,), out_specs=spec, check_vma=False)
```

```python
import jax
import jax.numpy as jnp
from jax import lax
from jax.sharding import PartitionSpec as P

AXES = ("row", "col", "mat")
N = 8
MIXED = False
SUM_TYPE = jnp.bfloat16
ORDER = (0, 1, 7, 2, 6, 3, 5, 4)
F32, BF16 = jnp.float32, jnp.bfloat16
ROWS_BY_ROWS = (((1,), (1,)), ((), ()))
COLS_BY_COLS = (((0,), (0,)), ((), ()))


def ring_to_col(p):
    return p if p < 4 else 11 - p


def place(mat, r, q):
    if MIXED and mat % 2 == 1:
        r, q = q, r
    return (r * 8 + ring_to_col(q)) * 4 + mat


def shift(x, axis, by):
    dr, dq = (by, 0) if axis == "r" else (0, by)
    pairs = [
        (place(m, r, q), place(m, (r + dr) % N, (q + dq) % N))
        for m in range(4)
        for r in range(N)
        for q in range(N)
    ]
    return lax.ppermute(x, AXES, pairs)


def dot(a, b, dims=(((1,), (0,)), ((), ()))):
    return lax.dot_general(a, b, dims, preferred_element_type=F32)


def ring_gather(x, axis):
    by = 1 if x.shape[1] > 128 else 0
    half = x.shape[by] // 2
    out = [None] * N
    out[0] = x
    up, down = x, x
    for s in (1, 2, 3):
        up = shift(up, axis, 1)
        down = shift(down, axis, -1)
        out[N - s] = up
        out[s] = down
    first = shift(lax.slice_in_dim(up, 0, half, axis=by), axis, 1)
    second = shift(lax.slice_in_dim(down, half, 2 * half, axis=by), axis, -1)
    out[4] = jnp.concatenate([first, second], by)
    return out


def pack(x):
    n, w = x.shape
    full, rest = w // 128, w % 128
    if rest != 64:
        return x
    tail = x[:, full * 128 :]
    tail = jnp.concatenate([tail[: n // 2], tail[n // 2 :]], 1)
    return jnp.concatenate([x[:, i * 128 : (i + 1) * 128] for i in range(full)] + [tail], 0)


def unpack(x, n, w):
    full, rest = w // 128, w % 128
    if rest != 64:
        return x
    tail = x[full * n :]
    tail = jnp.concatenate([tail[:, :64], tail[:, 64:]], 0)
    return jnp.concatenate([x[i * n : (i + 1) * n] for i in range(full)] + [tail], 1)


def ring_gather_tile(x, axis):
    n, w = x.shape
    got = ring_gather(pack(x), axis)
    return [x] + [unpack(g, n, w) for g in got[1:]]


def ring_sum(last, factor, terms, axis):
    half = last.shape[1] // 2

    def sent(x, by):
        return shift(x.astype(SUM_TYPE), axis, by)

    first, second = sent(last[:, :half], 1), sent(last[:, half:], -1)
    first, second, factor = lax.optimization_barrier((first, second, factor))
    term = terms(factor)
    up, down = term[3], term[5]
    up = jnp.concatenate([up[:, :half] + first.astype(F32), up[:, half:]], 1)
    down = jnp.concatenate([down[:, :half], down[:, half:] + second.astype(F32)], 1)
    for d in (2, 1):
        up = sent(up, 1).astype(F32) + term[d]
        down = sent(down, -1).astype(F32) + term[N - d]
    return term[0] + sent(up, 1).astype(F32) + sent(down, -1).astype(F32)


def body(iterate):
    m, cols = iterate.shape
    size = N * m
    z = lax.axis_index("row")
    col = lax.axis_index("col")
    ring = jnp.where(col < 4, col, 11 - col)
    if MIXED:
        odd = lax.axis_index("mat") % 2 == 1
        r = jnp.where(odd, ring, z)
        q = jnp.where(odd, z, ring)
    else:
        r, q = z, ring

    arrival = lax.broadcasted_iota(jnp.int32, (N, m, size), 0)
    distance = jnp.zeros_like(arrival)
    for p, d in enumerate(ORDER):
        distance = jnp.where(arrival == p, d, distance)
    row = lax.broadcasted_iota(jnp.int32, (N, m, size), 1)
    target = lax.broadcasted_iota(jnp.int32, (N, m, size), 2)

    def turn(at):
        return ((distance + at) % N * m + row == target).astype(BF16).reshape(size, size)

    turn_q, turn_r = lax.optimization_barrier((turn(q), turn(r)))
    over_q = ring_gather(iterate, "q")
    over_r = ring_gather(iterate, "r")
    seven = 7 * m
    space = jnp.zeros((m, cols), BF16)
    right = jnp.concatenate([over_q[d] for d in ORDER[:7]] + [space], 0)
    left = jnp.concatenate([over_r[d] for d in ORDER[:7]] + [space], 0)
    most = dot(left[:seven], right[:seven], ROWS_BY_ROWS)
    right = lax.dynamic_update_slice(right, over_q[4], (seven, 0))
    left = lax.dynamic_update_slice(left, over_r[4], (seven, 0))
    side = dot(left[:seven], over_q[4], ROWS_BY_ROWS)
    below = dot(over_r[4], right, ROWS_BY_ROWS)
    tile = jnp.concatenate([jnp.concatenate([most, side], 1), below], 0)
    tile = (tile * (1.0 / cols)).astype(BF16)

    tile_q = dot(tile, turn_q).astype(BF16)
    turned = dot(tile, turn_r, COLS_BY_COLS).astype(BF16)
    gram = dot(turned, turn_q, COLS_BY_COLS).astype(BF16)

    gram_q = ring_gather_tile(tile_q, "q")
    gram_r = ring_gather_tile(turned, "r")
    stack = jnp.stack([gram_q[d].reshape(N, m, size) for d in ORDER], 1).reshape(N, size, size)
    square = jnp.zeros((size, size), F32)
    for p, d in enumerate(ORDER):
        square = square + dot(gram_r[d], stack[p], COLS_BY_COLS)
    poly = (-4.775 * gram.astype(F32) + 2.0315 * square).astype(BF16)
    poly = lax.optimization_barrier(poly)
    poly = dot(turn_r, poly).astype(BF16)
    poly_r = dot(poly, turn_q, ROWS_BY_ROWS).astype(BF16)
    poly_q = dot(turn_q, poly, ROWS_BY_ROWS).astype(BF16)

    split = cols // 2

    def terms(a, x):
        pairs = [dot(a[p * m : (p + 2) * m], x) for p in (5, 3, 1)]
        made = {0: dot(a[:m], x)}
        for p, y in zip((5, 3, 1), pairs):
            made[ORDER[p]], made[ORDER[p + 1]] = y[:m], y[m:]
        return made

    def summed(a, x, axis):
        return ring_sum(dot(a[7 * m :], x), a, lambda a: terms(a, x), axis)

    product = jnp.concatenate(
        [summed(poly_q, left[:, :split], "q"), summed(poly_r, right[:, split:], "r")], 1
    )
    return (3.4445 * iterate.astype(F32) + product).astype(BF16)


def solution(mesh):
    spec = P(("mat", "row", "col"), None)
    return jax.shard_map(body, mesh=mesh, in_specs=(spec,), out_specs=spec, check_vma=False)
```

```python
import jax
import jax.numpy as jnp
from jax import lax
from jax.sharding import PartitionSpec as P

AXES = ("row", "col", "mat")
N = 8
MIXED = False
SUM_TYPE = jnp.bfloat16
ORDER = (0, 1, 7, 2, 6, 3, 5, 4)
F32, BF16 = jnp.float32, jnp.bfloat16
ROWS_BY_ROWS = (((1,), (1,)), ((), ()))
COLS_BY_COLS = (((0,), (0,)), ((), ()))


def ring_to_col(p):
    return p if p < 4 else 11 - p


def place(mat, r, q):
    if MIXED and mat % 2 == 1:
        r, q = q, r
    return (r * 8 + ring_to_col(q)) * 4 + mat


def shift(x, axis, by):
    dr, dq = (by, 0) if axis == "r" else (0, by)
    pairs = [
        (place(m, r, q), place(m, (r + dr) % N, (q + dq) % N))
        for m in range(4)
        for r in range(N)
        for q in range(N)
    ]
    return lax.ppermute(x, AXES, pairs)


def dot(a, b, dims=(((1,), (0,)), ((), ()))):
    return lax.dot_general(a, b, dims, preferred_element_type=F32)


def ring_gather(x, axis):
    by = 1 if x.shape[1] > 128 else 0
    half = x.shape[by] // 2
    out = [None] * N
    out[0] = x
    up, down = x, x
    for s in (1, 2, 3):
        up = shift(up, axis, 1)
        down = shift(down, axis, -1)
        out[N - s] = up
        out[s] = down
    first = shift(lax.slice_in_dim(up, 0, half, axis=by), axis, 1)
    second = shift(lax.slice_in_dim(down, half, 2 * half, axis=by), axis, -1)
    out[4] = jnp.concatenate([first, second], by)
    return out


def pack(x):
    n, w = x.shape
    full, rest = w // 128, w % 128
    if rest != 64:
        return x
    tail = x[:, full * 128 :]
    tail = jnp.concatenate([tail[: n // 2], tail[n // 2 :]], 1)
    return jnp.concatenate([x[:, i * 128 : (i + 1) * 128] for i in range(full)] + [tail], 0)


def unpack(x, n, w):
    full, rest = w // 128, w % 128
    if rest != 64:
        return x
    tail = x[full * n :]
    tail = jnp.concatenate([tail[:, :64], tail[:, 64:]], 0)
    return jnp.concatenate([x[i * n : (i + 1) * n] for i in range(full)] + [tail], 1)


def ring_gather_tile(x, axis):
    n, w = x.shape
    got = ring_gather(pack(x), axis)
    return [x] + [unpack(g, n, w) for g in got[1:]]


def ring_sum(last, factor, terms, axis):
    half = last.shape[1] // 2

    def sent(x, by):
        return shift(x.astype(SUM_TYPE), axis, by)

    first, second = sent(last[:, :half], 1), sent(last[:, half:], -1)
    first, second, factor = lax.optimization_barrier((first, second, factor))
    term = terms(factor)
    up, down = term[3], term[5]
    up = jnp.concatenate([up[:, :half] + first.astype(F32), up[:, half:]], 1)
    down = jnp.concatenate([down[:, :half], down[:, half:] + second.astype(F32)], 1)
    for d in (2, 1):
        up = sent(up, 1).astype(F32) + term[d]
        down = sent(down, -1).astype(F32) + term[N - d]
    return term[0] + sent(up, 1).astype(F32) + sent(down, -1).astype(F32)


def body(iterate):
    m, cols = iterate.shape
    size = N * m
    z = lax.axis_index("row")
    col = lax.axis_index("col")
    ring = jnp.where(col < 4, col, 11 - col)
    if MIXED:
        odd = lax.axis_index("mat") % 2 == 1
        r = jnp.where(odd, ring, z)
        q = jnp.where(odd, z, ring)
    else:
        r, q = z, ring

    arrival = lax.broadcasted_iota(jnp.int32, (N, m, size), 0)
    distance = jnp.zeros_like(arrival)
    for p, d in enumerate(ORDER):
        distance = jnp.where(arrival == p, d, distance)
    row = lax.broadcasted_iota(jnp.int32, (N, m, size), 1)
    target = lax.broadcasted_iota(jnp.int32, (N, m, size), 2)

    def turn(at):
        return ((distance + at) % N * m + row == target).astype(BF16).reshape(size, size)

    turn_q, turn_r = lax.optimization_barrier((turn(q), turn(r)))
    over_q = ring_gather(iterate, "q")
    over_r = ring_gather(iterate, "r")
    seven = 7 * m
    space = jnp.zeros((m, cols), BF16)
    right = jnp.concatenate([over_q[d] for d in ORDER[:7]] + [space], 0)
    left = jnp.concatenate([over_r[d] for d in ORDER[:7]] + [space], 0)
    most = dot(left[:seven], right[:seven], ROWS_BY_ROWS)
    right = lax.dynamic_update_slice(right, over_q[4], (seven, 0))
    left = lax.dynamic_update_slice(left, over_r[4], (seven, 0))
    side = dot(left[:seven], over_q[4], ROWS_BY_ROWS)
    below = dot(over_r[4], right, ROWS_BY_ROWS)
    tile = jnp.concatenate([jnp.concatenate([most, side], 1), below], 0)
    tile = (tile * (1.0 / cols)).astype(BF16)

    tile_q = dot(tile, turn_q).astype(BF16)
    turned = dot(tile, turn_r, COLS_BY_COLS).astype(BF16)
    gram = dot(turned, turn_q, COLS_BY_COLS).astype(BF16)

    gram_q = ring_gather_tile(tile_q, "q")
    gram_r = ring_gather_tile(turned, "r")
    stack = jnp.stack([gram_q[d].reshape(N, m, size) for d in ORDER], 1).reshape(N, size, size)
    square = jnp.zeros((size, size), F32)
    for p, d in enumerate(ORDER):
        square = square + dot(gram_r[d], stack[p], COLS_BY_COLS)
    poly = (-4.775 * gram.astype(F32) + 2.0315 * square).astype(BF16)
    poly = lax.optimization_barrier(poly)
    poly = dot(turn_r, poly).astype(BF16)
    poly_r = dot(poly, turn_q, ROWS_BY_ROWS).astype(BF16)
    poly_q = dot(turn_q, poly, ROWS_BY_ROWS).astype(BF16)

    split = cols * 9 // 16

    def terms(a, x):
        pairs = [dot(a[p * m : (p + 2) * m], x) for p in (5, 3, 1)]
        made = {0: dot(a[:m], x)}
        for p, y in zip((5, 3, 1), pairs):
            made[ORDER[p]], made[ORDER[p + 1]] = y[:m], y[m:]
        return made

    def summed(a, x, axis):
        return ring_sum(dot(a[7 * m :], x), a, lambda a: terms(a, x), axis)

    scaled = 3.4445 * iterate.astype(F32)
    over_q = (scaled[:, :split] + summed(poly_q, left[:, :split], "q")).astype(BF16)
    over_r = (scaled[:, split:] + summed(poly_r, right[:, split:], "r")).astype(BF16)
    return jnp.concatenate([over_q, over_r], 1)


def solution(mesh):
    spec = P(("mat", "row", "col"), None)
    return jax.shard_map(body, mesh=mesh, in_specs=(spec,), out_specs=spec, check_vma=False)
```

```python
import jax
import jax.numpy as jnp
from jax import lax
from jax.sharding import PartitionSpec as P

AXES = ("row", "col", "mat")
N = 8
MIXED = False
SUM_TYPE = jnp.bfloat16
ORDER = (0, 1, 7, 2, 6, 3, 5, 4)
F32, BF16 = jnp.float32, jnp.bfloat16
ROWS_BY_ROWS = (((1,), (1,)), ((), ()))
COLS_BY_COLS = (((0,), (0,)), ((), ()))


def ring_to_col(p):
    return p if p < 4 else 11 - p


def place(mat, r, q):
    if MIXED and mat % 2 == 1:
        r, q = q, r
    return (r * 8 + ring_to_col(q)) * 4 + mat


def shift(x, axis, by):
    dr, dq = (by, 0) if axis == "r" else (0, by)
    pairs = [
        (place(m, r, q), place(m, (r + dr) % N, (q + dq) % N))
        for m in range(4)
        for r in range(N)
        for q in range(N)
    ]
    return lax.ppermute(x, AXES, pairs)


def dot(a, b, dims=(((1,), (0,)), ((), ()))):
    return lax.dot_general(a, b, dims, preferred_element_type=F32)


def ring_gather(x, axis):
    by = 1 if x.shape[1] > 128 else 0
    half = x.shape[by] // 2
    out = [None] * N
    out[0] = x
    up, down = x, x
    for s in (1, 2, 3):
        up = shift(up, axis, 1)
        down = shift(down, axis, -1)
        out[N - s] = up
        out[s] = down
    first = shift(lax.slice_in_dim(up, 0, half, axis=by), axis, 1)
    second = shift(lax.slice_in_dim(down, half, 2 * half, axis=by), axis, -1)
    out[4] = jnp.concatenate([first, second], by)
    return out


def pack(x):
    n, w = x.shape
    full, rest = w // 128, w % 128
    if rest != 64:
        return x
    tail = x[:, full * 128 :]
    tail = jnp.concatenate([tail[: n // 2], tail[n // 2 :]], 1)
    return jnp.concatenate([x[:, i * 128 : (i + 1) * 128] for i in range(full)] + [tail], 0)


def unpack(x, n, w):
    full, rest = w // 128, w % 128
    if rest != 64:
        return x
    tail = x[full * n :]
    tail = jnp.concatenate([tail[:, :64], tail[:, 64:]], 0)
    return jnp.concatenate([x[i * n : (i + 1) * n] for i in range(full)] + [tail], 1)


def ring_gather_tile(x, axis):
    n, w = x.shape
    got = ring_gather(pack(x), axis)
    return [x] + [unpack(g, n, w) for g in got[1:]]


def ring_sum(last, factor, terms, axis):
    half = last.shape[1] // 2

    def sent(x, by):
        return shift(x.astype(SUM_TYPE), axis, by)

    first, second = sent(last[:, :half], 1), sent(last[:, half:], -1)
    first, second, factor = lax.optimization_barrier((first, second, factor))
    term = terms(factor)
    up, down = term[3], term[5]
    up = jnp.concatenate([up[:, :half] + first.astype(F32), up[:, half:]], 1)
    down = jnp.concatenate([down[:, :half], down[:, half:] + second.astype(F32)], 1)
    for d in (2, 1):
        up = sent(up, 1).astype(F32) + term[d]
        down = sent(down, -1).astype(F32) + term[N - d]
    return term[0] + sent(up, 1).astype(F32) + sent(down, -1).astype(F32)


def body(iterate):
    m, cols = iterate.shape
    size = N * m
    z = lax.axis_index("row")
    col = lax.axis_index("col")
    ring = jnp.where(col < 4, col, 11 - col)
    if MIXED:
        odd = lax.axis_index("mat") % 2 == 1
        r = jnp.where(odd, ring, z)
        q = jnp.where(odd, z, ring)
    else:
        r, q = z, ring

    arrival = lax.broadcasted_iota(jnp.int32, (N, m, size), 0)
    distance = jnp.zeros_like(arrival)
    for p, d in enumerate(ORDER):
        distance = jnp.where(arrival == p, d, distance)
    row = lax.broadcasted_iota(jnp.int32, (N, m, size), 1)
    target = lax.broadcasted_iota(jnp.int32, (N, m, size), 2)

    def turn(at):
        return ((distance + at) % N * m + row == target).astype(BF16).reshape(size, size)

    turn_q, turn_r = lax.optimization_barrier((turn(q), turn(r)))
    over_q = ring_gather(iterate, "q")
    over_r = ring_gather(iterate, "r")
    seven = 7 * m
    space = jnp.zeros((m, cols), BF16)
    right = jnp.concatenate([over_q[d] for d in ORDER[:7]] + [space], 0)
    left = jnp.concatenate([over_r[d] for d in ORDER[:7]] + [space], 0)
    most = dot(left[:seven], right[:seven], ROWS_BY_ROWS)
    right = lax.dynamic_update_slice(right, over_q[4], (seven, 0))
    left = lax.dynamic_update_slice(left, over_r[4], (seven, 0))
    side = dot(left[:seven], over_q[4], ROWS_BY_ROWS)
    below = dot(over_r[4], right, ROWS_BY_ROWS)
    tile = jnp.concatenate([jnp.concatenate([most, side], 1), below], 0)
    tile = (tile * (1.0 / cols)).astype(BF16)

    tile_q = dot(tile, turn_q).astype(BF16)
    turned = dot(tile, turn_r, COLS_BY_COLS).astype(BF16)
    gram = dot(turned, turn_q, COLS_BY_COLS).astype(BF16)

    gram_q = ring_gather_tile(tile_q, "q")
    gram_r = ring_gather_tile(turned, "r")
    stack = jnp.stack([gram_q[d].reshape(N, m, size) for d in ORDER], 1).reshape(N, size, size)
    square = jnp.zeros((size, size), F32)
    for p, d in enumerate(ORDER):
        square = square + dot(gram_r[d], stack[p], COLS_BY_COLS)
    poly = (-4.775 * gram.astype(F32) + 2.0315 * square).astype(BF16)
    poly = lax.optimization_barrier(poly)
    poly = dot(turn_r, poly).astype(BF16)
    poly_r = dot(poly, turn_q, ROWS_BY_ROWS).astype(BF16)
    poly_q = dot(turn_q, poly, ROWS_BY_ROWS).astype(BF16)

    split = cols // 2

    def terms(a, x):
        pairs = [dot(a[p * m : (p + 2) * m], x) for p in (5, 3, 1)]
        made = {0: dot(a[:m], x)}
        for p, y in zip((5, 3, 1), pairs):
            made[ORDER[p]], made[ORDER[p + 1]] = y[:m], y[m:]
        return made

    def summed(a, x, axis):
        return ring_sum(dot(a[7 * m :], x), a, lambda a: terms(a, x), axis)

    product = jnp.concatenate(
        [summed(poly_r, right[:, :split], "r"), summed(poly_q, left[:, split:], "q")], 1
    )
    return (3.4445 * iterate.astype(F32) + product).astype(BF16)


def solution(mesh):
    spec = P(("mat", "row", "col"), None)
    return jax.shard_map(body, mesh=mesh, in_specs=(spec,), out_specs=spec, check_vma=False)
```
